256 devices in a mesh: rep: 8 (over z_lo, y), fsdp: 32 (over z_hi, x, core).
Axes of the slice: x: 4, y: 4, z: 8 (z_hi: 4, z_lo: 2; z = z_hi * 2 + z_lo), core: 2. Of those that a mesh axis runs over, the one named last changes fastest.
Arguments:
- activations: bfloat16 [131072, 4096], P(('rep', 'fsdp')), may hold values from -6 to 6
- norm_gain: float32 [8, 4096], P('rep', 'fsdp'), may hold values from 0.5 to 1.5
- key_weight: float32 [8, 4096, 512], P('rep', 'fsdp'), may hold values from -6 to 6
- value_weight: float32 [8, 4096, 512], P('rep', 'fsdp'), may hold values from -6 to 6
- key_cotangent: bfloat16 [131072, 512], P(('rep', 'fsdp')), may hold values from -6 to 6
- value_cotangent: bfloat16 [131072, 512], P(('rep', 'fsdp')), may hold values from -6 to 6
- step_index: int32 [1], replicated, may hold values from 0 to 63
- plan: int32 [8], replicated, may hold values from 0 to 7, as said below
Outputs:
- keys: bfloat16 [131072, 512], P(('rep', 'fsdp'))
- values: bfloat16 [131072, 512], P(('rep', 'fsdp'))
- input_grad: bfloat16 [131072, 4096], P(('rep', 'fsdp'))
- new_key_weight: float32 [8, 4096, 512], P('rep', 'fsdp')
- new_value_weight: float32 [8, 4096, 512], P('rep', 'fsdp')
- new_gain: float32 [8, 4096], P('rep', 'fsdp')
The draws below stay inside these ranges and needn't reach their ends.
Inputs may be any that keep to these rules, and one draw needn't show every extreme that they name: `plan`: each entry is a partner mask, 0 meaning no partner; every value from 0 to 7 appears.
All inputs are finite; a program needn't handle non-finite values.
Results may differ from the reference program's by a relative error of at most 0.0095.
Values may be sent and summed in bfloat16 or wider, within the bound.
A program may use at most 128 MiB of HBM per device.

```python
import math
import jax
import jax.numpy as jnp
from jax import lax

D = 4096
KVW = 512
TOK_DEV = 512
HOPS = 8
TOKENS = 131072
N_REP = 8
N_FSDP = 32


def draw_plan(key, part):
    key = jax.random.fold_in(key, 11)
    order_key, offset_key = jax.random.split(key)
    order = jax.random.permutation(order_key, HOPS).astype(jnp.int32)
    offset = jax.random.randint(offset_key, (), 0, N_REP, dtype=jnp.int32)
    return ((order + offset) % N_REP).astype(jnp.int32)


def level_of(own_key, extent, shards, low, top_value):
    gain, own = 1.0, jax.random.fold_in(own_key, 6)
    for axis_at, parts in shards:
        draws = jnp.exp(jax.random.uniform(jax.random.fold_in(own, axis_at), (parts,), jnp.float32, low / len(shards), top_value / len(shards)))
        gain = gain * jnp.repeat(draws, extent[axis_at] // parts).reshape([-1 if axis == axis_at else 1 for axis in range(len(extent))])
    return gain


def scatter_about(rng, extent, scale, reach, shards=(), kind=jnp.bfloat16):
    result = jax.random.normal(rng, extent, jnp.float32) * scale
    if len(shards) > 0:
        result = level_of(rng, extent, shards, -0.22, 0.18) * result
    return jnp.clip(result, min=-reach, max=reach).astype(kind)


def setup_inputs(seed: int = 0) -> dict:
    seeds = jax.random.split(jax.random.key(seed), 9)
    activations = scatter_about(seeds[0], (TOKENS, D), 1.0, 6.0, ((0, 256),))
    norm_gain = jnp.clip(1.0 + 0.1 * jax.random.normal(seeds[1], (N_REP, D), jnp.float32), 0.5, 1.5)
    key_weight = scatter_about(seeds[2], (N_REP, D, KVW), 1.0, 6.0, ((0, 8), (1, 32)), jnp.float32)
    value_weight = scatter_about(seeds[3], (N_REP, D, KVW), 1.0, 6.0, ((0, 8), (1, 32)), jnp.float32)
    key_cotangent = scatter_about(seeds[4], (TOKENS, KVW), 1.0, 6.0, ((0, 256),))
    value_cotangent = scatter_about(seeds[5], (TOKENS, KVW), 1.0, 6.0, ((0, 256),))
    step_index = jax.random.randint(seeds[6], (1,), 0, 64).astype(jnp.int32)
    plan = draw_plan(jax.random.fold_in(seeds[8], 71), 0)
    return {"activations": activations, "norm_gain": norm_gain, "key_weight": key_weight, "value_weight": value_weight, "key_cotangent": key_cotangent, "value_cotangent": value_cotangent, "step_index": step_index, "plan": plan}


lr_weight = 0.25
lr_gain = 0.005

def reference(activations, norm_gain, key_weight, value_weight, key_cotangent, value_cotangent, step_index, plan):
    group_rows = TOK_DEV * N_FSDP
    root_inv = 1.0 / math.sqrt(D)
    keys_list, values_list, grad_list = ([], [], [])
    upd_key, upd_value, upd_gain = ([], [], [])
    for group in range(N_REP):
        widened = activations[group * group_rows:(group + 1) * group_rows].astype(jnp.float32)
        key_grad_in = key_cotangent[group * group_rows:(group + 1) * group_rows]
        value_grad_in = value_cotangent[group * group_rows:(group + 1) * group_rows]
        gain_b = norm_gain[group].astype(jnp.bfloat16)
        key_b = key_weight[group].astype(jnp.bfloat16)
        value_b = value_weight[group].astype(jnp.bfloat16)
        inv_rms = lax.rsqrt(lax.optimization_barrier(jnp.mean(widened * widened, axis=-1, keepdims=True)) + 1e-05)
        normed = widened * inv_rms
        normed_b = (normed * gain_b).astype(jnp.bfloat16)
        keys_list.append((jnp.dot(normed_b, key_b, preferred_element_type=jnp.float32) * root_inv).astype(jnp.bfloat16))
        values_list.append((jnp.dot(normed_b, value_b, preferred_element_type=jnp.float32) * root_inv).astype(jnp.bfloat16))
        dnormed_in = (jnp.dot(key_grad_in, key_b.T, preferred_element_type=jnp.float32) + jnp.dot(value_grad_in, value_b.T, preferred_element_type=jnp.float32)) * root_inv
        dnormed = dnormed_in * gain_b
        inner = lax.optimization_barrier(jnp.mean(dnormed * normed, axis=-1, keepdims=True))
        grad_list.append((inv_rms * (dnormed - normed * inner)).astype(jnp.bfloat16))
        normed_runs = normed_b.reshape(N_FSDP, TOK_DEV, D).astype(jnp.float32)
        key_runs = key_grad_in.reshape(N_FSDP, TOK_DEV, KVW).astype(jnp.float32)
        value_runs = value_grad_in.reshape(N_FSDP, TOK_DEV, KVW).astype(jnp.float32)
        key_part = (jnp.einsum('ftd,ftk->fdk', normed_runs, key_runs) * root_inv).astype(jnp.bfloat16)
        value_part = (jnp.einsum('ftd,ftk->fdk', normed_runs, value_runs) * root_inv).astype(jnp.bfloat16)
        gain_part = lax.optimization_barrier(jnp.sum((dnormed_in * normed).reshape(N_FSDP, TOK_DEV, D), axis=1)).astype(jnp.bfloat16)
        key_total = lax.optimization_barrier(jnp.sum(key_part.astype(jnp.float32), axis=0))
        value_total = lax.optimization_barrier(jnp.sum(value_part.astype(jnp.float32), axis=0))
        gain_total = lax.optimization_barrier(jnp.sum(gain_part.astype(jnp.float32), axis=0))
        upd_key.append(key_weight[group] - lr_weight * key_total)
        upd_value.append(value_weight[group] - lr_weight * value_total)
        upd_gain.append(norm_gain[group] - lr_gain * gain_total)
    upd_key = jnp.stack(upd_key)
    upd_value = jnp.stack(upd_value)
    upd_gain = jnp.stack(upd_gain)
    hop_mask = plan[step_index[0] % HOPS]
    partner = jnp.bitwise_xor(jnp.arange(N_REP, dtype=jnp.int32), hop_mask.astype(jnp.int32))
    new_key = (upd_key + upd_key[partner]) * 0.5
    new_value = (upd_value + upd_value[partner]) * 0.5
    new_gain = (upd_gain + upd_gain[partner]) * 0.5
    return (jnp.concatenate(keys_list, axis=0), jnp.concatenate(values_list, axis=0), jnp.concatenate(grad_list, axis=0), new_key, new_value, new_gain)
```

```python
import functools

import jax
import jax.numpy as jnp
from jax import lax
from jax.experimental import pallas as pl
from jax.experimental.pallas import tpu as pltpu
from jax.sharding import PartitionSpec as P

MESH = pl.DeviceIdType.MESH
F32 = jnp.float32
BF16 = jnp.bfloat16

lr_weight = 0.25
lr_gain = 0.005

NX = 4
NZ = 4
N_SEND = 96


def kernel(
    act,
    gain_ref,
    kw,
    vw,
    kc,
    vc,
    step_ref,
    plan_ref,
    keys_ref,
    values_ref,
    dn_out,
    coef_ref,
    nk_ref,
    nv_ref,
    ng_ref,
    xv,
    x2h,
    ctv,
    ctT,
    wv,
    gw,
    gs,
    ropp,
    rpl,
    rsm,
    zs,
    rz,
    acc,
    dnb,
    inv_ref,
    own,
    psend,
    precv,
    ssem,
    lsem,
    xsem,
    ctsem,
    agsem,
    sibsem,
    oppsem,
    plsem,
    smsem,
    zsem,
    psem,
    dsem,
):
    me = lax.axis_index("fsdp")
    rep = lax.axis_index("rep")
    zh = me // 8
    xx = (me // 2) % 4
    c = me % 2
    sib = 1 - c

    def at(dz, dx):
        return lax.rem(zh + dz, NZ) * NX + lax.rem(xx + dx, NX)

    def dev(dz, dx, core):
        return (rep, at(dz, dx) * 2 + core)

    sibling = dev(0, 0, sib)
    right = dev(0, 1, c)
    left = dev(0, 3, c)
    partners = [
        (rep + 1 - 2 * (rep % 2), me),
        (rep + 2 - 4 * ((rep // 2) % 2), me),
        (rep + 4 - 8 * ((rep // 4) % 2), me),
    ]
    sends = []

    def send(src, dst, sem, to):
        cp = pltpu.make_async_remote_copy(
            src_ref=src,
            dst_ref=dst,
            send_sem=ssem.at[len(sends)],
            recv_sem=sem,
            device_id=to,
            device_id_type=MESH,
        )
        cp.start()
        sends.append(cp)

    def arrived(dst, sem):
        pltpu.make_async_remote_copy(
            src_ref=dst,
            dst_ref=dst,
            send_sem=ssem.at[0],
            recv_sem=sem,
            device_id=sibling,
            device_id_type=MESH,
        ).wait_recv()

    def local(src, dst, i):
        return pltpu.make_async_copy(src, dst, lsem.at[i])

    l_kw = local(kw.at[0], wv.at[:, pl.ds(0, 512)], 0)
    l_vw = local(vw.at[0], wv.at[:, pl.ds(512, 512)], 1)
    l_x = local(act, xv, 2)
    l_kc = local(kc, ctv.at[:, pl.ds(0, 512)], 3)
    l_vc = local(vc, ctv.at[:, pl.ds(512, 512)], 4)
    for cp in (l_kw, l_vw, l_x, l_kc, l_vc):
        cp.start()

    bar = pltpu.get_barrier_semaphore()
    peers = [sibling, right, left, dev(1, 0, c), dev(2, 0, c), dev(3, 0, c)] + partners
    for to in peers:
        pl.semaphore_signal(bar, inc=1, device_id=to, device_id_type=MESH)
    l_own = []
    for s in (2, 1, 3, 0):
        tx = lax.rem(xx + s, NX)
        for z in range(NZ):
            col = pl.multiple_of(((z * NX + tx) * 2 + c) * 128, 128)
            cp = local(
                act.at[:, pl.ds(col, 128)],
                x2h.at[s, pl.ds(pl.multiple_of(c * 512, 512), 512), pl.ds(z * 128, 128)],
                5 + s * 4 + z,
            )
            cp.start()
            l_own.append(cp)
    pl.semaphore_wait(bar, len(peers))

    l_kw.wait()
    l_vw.wait()
    gain_row = gain_ref[...]
    gain_col = jnp.transpose(jnp.broadcast_to(gain_row, (128, 128)))[:, 0:1]
    mine = gw.at[at(0, 0), pl.ds(pl.multiple_of(c * 128, 128), 128), :]
    mine[...] = (wv[...] * gain_col).astype(BF16)

    def piece(dz, dx):
        return gw.at[at(dz, dx), pl.ds(pl.multiple_of(c * 128, 128), 128), :]

    def sib_piece(dz, dx):
        return gw.at[at(dz, dx), pl.ds(pl.multiple_of(sib * 128, 128), 128), :]

    send(piece(0, 0), piece(0, 0), agsem.at[3], right)
    send(piece(0, 0), piece(0, 0), agsem.at[1], left)
    for dz in (1, 3, 2):
        send(piece(0, 0), piece(0, 0), agsem.at[(4 - dz) * 4], dev(dz, 0, c))

    for s in (2, 1, 3, 0):
        tx = lax.rem(xx + s, NX)
        for z in range(NZ):
            col = pl.multiple_of(((z * NX + tx) * 2 + sib) * 128, 128)
            send(
                act.at[:, pl.ds(col, 128)],
                x2h.at[s, pl.ds(pl.multiple_of(c * 512, 512), 512), pl.ds(z * 128, 128)],
                xsem.at[s],
                sibling,
            )
    send(piece(0, 0), piece(0, 0), sibsem.at[0], sibling)

    l_x.wait()
    l_kc.wait()
    l_vc.wait()

    @pl.loop(0, 4)
    def _(b):
        rows = pl.ds(pl.multiple_of(b * 128, 128), 128)
        xb = xv[rows, :].astype(F32)
        ms = jnp.sum(xb * xb, axis=-1, keepdims=True) * (1.0 / 4096.0)
        inv = lax.rsqrt(ms + 1e-05)
        inv_ref[rows, :] = jnp.broadcast_to(inv, (128, 128))
        lanes = pl.ds(pl.multiple_of(c * 512 + b * 128, 128), 128)
        for r in range(2):
            ct = ctv[rows, r * 512 : (r + 1) * 512].astype(F32) * inv
            ctT[r, :, lanes] = jnp.transpose(ct).astype(BF16)

    own_lanes = pl.ds(pl.multiple_of(c * 512, 512), 512)
    sib_lanes = pl.ds(pl.multiple_of(sib * 512, 512), 512)
    for r in range(2):
        send(ctT.at[r, :, own_lanes], ctT.at[r, :, own_lanes], ctsem.at[r], sibling)
    for cp in l_own:
        cp.wait()

    def grad_block(r, s):
        res = jnp.dot(ctT[r], x2h[s], preferred_element_type=F32)
        for z in range(NZ):
            gs[r, s, z] = res[:, z * 128 : (z + 1) * 128].astype(BF16)

    HA = pl.ds(0, 2)
    HB = pl.ds(2, 2)

    def send_opp(r):
        send(gs.at[r, 2, HA], ropp.at[r, 0], oppsem.at[r * 2], right)
        send(gs.at[r, 2, HB], ropp.at[r, 1], oppsem.at[r * 2 + 1], left)

    def send_plain(r):
        send(gs.at[r, 1, HB], rpl.at[r, 0], plsem.at[r * 2], right)
        send(gs.at[r, 3, HA], rpl.at[r, 1], plsem.at[r * 2 + 1], left)

    def send_summed(r):
        arrived(ropp.at[r, 0], oppsem.at[r * 2])
        for h in range(2):
            gs[r, 1, h] = (gs[r, 1, h].astype(F32) + ropp[r, 0, h].astype(F32)).astype(BF16)
        send(gs.at[r, 1, HA], rsm.at[r, 0], smsem.at[r * 2], right)
        arrived(ropp.at[r, 1], oppsem.at[r * 2 + 1])
        for h in range(2):
            gs[r, 3, 2 + h] = (gs[r, 3, 2 + h].astype(F32) + ropp[r, 1, h].astype(F32)).astype(BF16)
        send(gs.at[r, 3, HB], rsm.at[r, 1], smsem.at[r * 2 + 1], left)

    def x_total(r):
        arrived(rpl.at[r, 0], plsem.at[r * 2])
        arrived(rpl.at[r, 1], plsem.at[r * 2 + 1])
        arrived(rsm.at[r, 0], smsem.at[r * 2])
        arrived(rsm.at[r, 1], smsem.at[r * 2 + 1])
        for h in range(2):
            zs[r, h] = (
                gs[r, 0, h].astype(F32) + rsm[r, 0, h].astype(F32) + rpl[r, 1, h].astype(F32)
            ).astype(BF16)
            zs[r, 2 + h] = (
                gs[r, 0, 2 + h].astype(F32) + rpl[r, 0, h].astype(F32) + rsm[r, 1, h].astype(F32)
            ).astype(BF16)
        for dz in (2, 1, 3):
            send(
                zs.at[r, lax.rem(zh + dz, NZ)],
                rz.at[r, 3 - dz],
                zsem.at[r * 3 + 3 - dz],
                dev(dz, 0, c),
            )

    hop = plan_ref[lax.rem(step_ref[0], 8)]
    gain_part = []

    def update(r):
        total = zs[r, zh].astype(F32)
        for i in range(3):
            arrived(rz.at[r, i], zsem.at[r * 3 + i])
            total = total + rz[r, i].astype(F32)
        grad = jnp.transpose(total) * (1.0 / 64.0)
        w = wv[:, r * 512 : (r + 1) * 512]
        own[r, 0:128, :] = w - lr_weight * gain_col * grad
        gain_part.append(jnp.sum(w.astype(BF16).astype(F32) * grad, axis=-1, keepdims=True))
        if r == 0:
            own[r, 128:144, :] = jnp.zeros((16, 512), F32)
        else:
            gain_sum = jnp.transpose(
                jnp.broadcast_to(gain_part[0] + gain_part[1], (128, 128))
            )[0:1, :]
            new_gain = gain_row - lr_gain * gain_sum
            own[r, 128:144, :] = jnp.broadcast_to(jnp.concatenate([new_gain] * 4, axis=1), (16, 512))
        psend[r, 0] = own[r].astype(BF16)
        swap(r, 0)

    def swap(r, stage):
        send(psend.at[r, stage], precv.at[r, stage], psem.at[r * 3 + stage], partners[stage])

    def swapped(r, stage):
        arrived(precv.at[r, stage], psem.at[r * 3 + stage])
        use = jnp.right_shift(hop, stage) % 2 == 1
        v = jnp.where(use, precv[r, stage].astype(F32), psend[r, stage].astype(F32))
        if stage < 2:
            psend[r, stage + 1] = v.astype(BF16)
            swap(r, stage + 1)
        else:
            o = own[r]
            avg = 0.5 * (o + jnp.where(hop == 0, o, v))
            if r == 0:
                nk_ref[0] = avg[0:128]
            else:
                nv_ref[0] = avg[0:128]
                ng_ref[...] = avg[128:129, 0:128]

    def gathered(dz, dx):
        arrived(piece(dz, dx), agsem.at[dz * 4 + dx])
        send(piece(dz, dx), piece(dz, dx), sibsem.at[dz * 4 + dx], sibling)

    def pairs(first, items):
        for n, (dz, dx) in enumerate(items):
            arrived(sib_piece(dz, dx), sibsem.at[dz * 4 + dx])
        for n, (dz, dx) in enumerate(items):
            j = at(dz, dx)
            cols = pl.ds(pl.multiple_of(j * 256, 256), 256)

            @pl.loop(0, 2)
            def _(b):
                rows = pl.ds(pl.multiple_of(b * 256, 256), 256)
                part = jnp.dot(xv[rows, cols], gw[j], preferred_element_type=F32)
                if first and n == 0:
                    acc[rows, :] = part
                else:
                    acc[rows, :] += part
                d = lax.dot_general(
                    ctv[rows, :], gw[j], (((1,), (1,)), ((), ())), preferred_element_type=F32
                )
                dnb[rows, cols] = (d * (inv_ref[rows, 0:1] * (1.0 / 64.0))).astype(BF16)

            pltpu.make_async_copy(dnb.at[:, cols], dn_out.at[:, cols], dsem).start()

    arrived(ctT.at[0, :, sib_lanes], ctsem.at[0])
    for s in (2, 1, 3, 0):
        arrived(x2h.at[s, sib_lanes, :], xsem.at[s])
    grad_block(0, 2)
    send_opp(0)
    grad_block(0, 1)
    grad_block(0, 3)
    send_plain(0)
    arrived(ctT.at[1, :, sib_lanes], ctsem.at[1])
    grad_block(1, 2)
    grad_block(1, 1)
    grad_block(1, 3)
    grad_block(0, 0)
    grad_block(1, 0)
    send_summed(0)
    send_opp(1)
    send_plain(1)
    pairs(True, [(0, 0)])
    gathered(0, 1)
    gathered(0, 3)
    pairs(False, [(0, 1), (0, 3)])
    gathered(1, 0)
    gathered(3, 0)
    x_total(0)
    gathered(2, 0)
    send_summed(1)
    send(piece(0, 3), piece(0, 3), agsem.at[2], right)
    for dr, dl in ((1, 3), (3, 2), (2, 1)):
        send(piece(dr, 0), piece(dr, 0), agsem.at[dr * 4 + 3], right)
        send(piece(dl, 0), piece(dl, 0), agsem.at[dl * 4 + 1], left)
    pairs(False, [(1, 0), (3, 0), (2, 0)])
    update(0)
    swapped(0, 0)
    x_total(1)
    swapped(0, 1)
    swapped(0, 2)
    update(1)
    gathered(1, 3)
    send(piece(1, 3), piece(1, 3), agsem.at[4 + 2], right)
    gathered(3, 1)
    send(piece(3, 1), piece(3, 1), agsem.at[12 + 2], left)
    gathered(2, 1)
    send(piece(2, 1), piece(2, 1), agsem.at[8 + 2], left)
    gathered(0, 2)
    swapped(1, 0)
    pairs(False, [(1, 3), (3, 1), (2, 1), (0, 2)])
    swapped(1, 1)
    gathered(3, 3)
    gathered(2, 3)
    gathered(1, 1)
    pairs(False, [(3, 3), (2, 3), (1, 1)])
    swapped(1, 2)
    gathered(3, 2)
    gathered(1, 2)
    pairs(False, [(3, 2), (1, 2)])
    gathered(2, 2)
    pairs(False, [(2, 2)])

    @pl.loop(0, 4)
    def _(b):
        rows = pl.ds(pl.multiple_of(b * 128, 128), 128)
        inv = inv_ref[rows, 0:1]
        kv = acc[rows, :] * (inv * (1.0 / 64.0))
        inner = jnp.sum(kv * ctv[rows, :].astype(F32), axis=-1, keepdims=True) * (1.0 / 4096.0)
        keys_ref[rows, :] = kv[:, 0:512].astype(BF16)
        values_ref[rows, :] = kv[:, 512:1024].astype(BF16)
        coef_ref[rows, :] = jnp.broadcast_to(inv * inv * inner, (128, 128))

    for cp in sends:
        cp.wait_send()
    pltpu.make_async_copy(dnb, dn_out, dsem).wait()


def body(
    activations,
    norm_gain,
    key_weight,
    value_weight,
    key_cotangent,
    value_cotangent,
    step_index,
    plan,
):
    any_spec = pl.BlockSpec(memory_space=pl.ANY)
    vmem = pl.BlockSpec(memory_space=pltpu.VMEM)
    smem = pl.BlockSpec(memory_space=pltpu.SMEM)
    shape = jax.ShapeDtypeStruct
    V = pltpu.VMEM
    DMA = pltpu.SemaphoreType.DMA
    keys, values, dn, coef, nk, nv, ng = pl.pallas_call(
        kernel,
        name="group_step",
        out_shape=(
            shape((512, 512), BF16),
            shape((512, 512), BF16),
            shape((512, 4096), BF16),
            shape((512, 128), F32),
            shape((1, 128, 512), F32),
            shape((1, 128, 512), F32),
            shape((1, 128), F32),
        ),
        in_specs=[any_spec, vmem, any_spec, any_spec, any_spec, any_spec, smem, smem],
        out_specs=(vmem, vmem, any_spec, vmem, vmem, vmem, vmem),
        scratch_shapes=[
            V((512, 4096), BF16),
            V((4, 1024, 512), BF16),
            V((512, 1024), BF16),
            V((2, 512, 1024), BF16),
            V((128, 1024), F32),
            V((16, 256, 1024), BF16),
            V((2, 4, 4, 512, 128), BF16),
            V((2, 2, 2, 512, 128), BF16),
            V((2, 2, 2, 512, 128), BF16),
            V((2, 2, 2, 512, 128), BF16),
            V((2, 4, 512, 128), BF16),
            V((2, 3, 512, 128), BF16),
            V((512, 1024), F32),
            V((512, 4096), BF16),
            V((512, 128), F32),
            V((2, 144, 512), F32),
            V((2, 3, 144, 512), BF16),
            V((2, 3, 144, 512), BF16),
            DMA((N_SEND,)),
            DMA((24,)),
            DMA((4,)),
            DMA((2,)),
            DMA((16,)),
            DMA((16,)),
            DMA((4,)),
            DMA((4,)),
            DMA((4,)),
            DMA((6,)),
            DMA((6,)),
            DMA,
        ],
        compiler_params=pltpu.CompilerParams(
            collective_id=0, has_side_effects=True, vmem_limit_bytes=58 << 20
        ),
        cost_estimate=pl.CostEstimate(
            flops=13_000_000_000, bytes_accessed=24 << 20, transcendentals=512
        ),
    )(
        activations,
        norm_gain,
        key_weight,
        value_weight,
        key_cotangent,
        value_cotangent,
        step_index,
        plan,
    )
    input_grad = (dn.astype(F32) - activations.astype(F32) * coef[:, 0:1]).astype(BF16)
    return keys, values, input_grad, nk, nv, ng


def solution(mesh):
    in_specs = (
        P(("rep", "fsdp"), None),
        P("rep", "fsdp"),
        P("rep", "fsdp", None),
        P("rep", "fsdp", None),
        P(("rep", "fsdp"), None),
        P(("rep", "fsdp"), None),
        P(),
        P(),
    )
    out_specs = (
        P(("rep", "fsdp"), None),
        P(("rep", "fsdp"), None),
        P(("rep", "fsdp"), None),
        P("rep", "fsdp", None),
        P("rep", "fsdp", None),
        P("rep", "fsdp"),
    )
    return jax.shard_map(body, mesh=mesh, in_specs=in_specs, out_specs=out_specs, check_vma=False)
```

```python
import jax
import jax.numpy as jnp
from jax import lax
from jax.experimental import pallas as pl
from jax.experimental.pallas import tpu as pltpu
from jax.sharding import PartitionSpec as P

MESH = pl.DeviceIdType.MESH
F32 = jnp.float32
BF16 = jnp.bfloat16

lr_weight = 0.25
lr_gain = 0.005

FINISH = 8
FROWS = 512 // FINISH
NX = 4
NZ = 4
N_SEND = 128
ROUNDS = 4
KR = 1024 // ROUNDS


def kernel(
    act,
    gain_in,
    kw,
    vw,
    kc,
    vc,
    step_in,
    plan_in,
    keys_out,
    values_out,
    dn_out,
    coef_out,
    nk_out,
    nv_out,
    ng_out,
    keys_ref,
    values_ref,
    dn_ref,
    coef_ref,
    nw_ref,
    ng_ref,
    xv,
    x2h,
    ctv,
    ctT,
    wv,
    gw,
    gs,
    ropp,
    rpl,
    rsm,
    zs,
    rz,
    acc,
    gain_ref,
    step_ref,
    plan_ref,
    inv_ref,
    own,
    psend,
    precv,
    ssem,
    lsem,
    xsem,
    ctsem,
    agsem,
    agh,
    sibsem,
    oppsem,
    plsem,
    smsem,
    zsem,
    psem,
    dsem,
    osem,
):
    me = lax.axis_index("fsdp")
    rep = lax.axis_index("rep")
    zh = me // 8
    xx = (me // 2) % 4
    c = me % 2
    sib = 1 - c

    def at(dz, dx):
        return lax.rem(zh + dz, NZ) * NX + lax.rem(xx + dx, NX)

    def dev(dz, dx, core):
        return (rep, at(dz, dx) * 2 + core)

    sibling = dev(0, 0, sib)
    right = dev(0, 1, c)
    left = dev(0, 3, c)
    bit0, bit1, bit2 = rep % 2, (rep // 2) % 2, (rep // 4) % 2
    partners = [
        (rep + 1 - 2 * bit0, me),
        (rep + 2 - 4 * bit1, me),
        (rep + 3 - 2 * bit0 - 4 * bit1, me),
        (rep + 4 - 8 * bit2, me),
    ]
    sends = []

    def send(src, dst, sem, to):
        cp = pltpu.make_async_remote_copy(
            src_ref=src,
            dst_ref=dst,
            send_sem=ssem.at[len(sends)],
            recv_sem=sem,
            device_id=to,
            device_id_type=MESH,
        )
        cp.start()
        sends.append(cp)

    def arrived(dst, sem):
        pltpu.make_async_remote_copy(
            src_ref=dst,
            dst_ref=dst,
            send_sem=ssem.at[0],
            recv_sem=sem,
            device_id=sibling,
            device_id_type=MESH,
        ).wait_recv()

    def local(src, dst, i):
        return pltpu.make_async_copy(src, dst, lsem.at[i])

    l_kw = local(kw.at[0], wv.at[:, pl.ds(0, 512)], 0)
    l_vw = local(vw.at[0], wv.at[:, pl.ds(512, 512)], 1)
    l_x = local(act, xv, 2)
    l_kc = local(kc, ctv.at[:, pl.ds(0, 512)], 3)
    l_vc = local(vc, ctv.at[:, pl.ds(512, 512)], 4)
    l_gain = local(gain_in, gain_ref, 21)
    l_step = local(step_in, step_ref, 22)
    l_plan = local(plan_in, plan_ref, 23)
    for cp in (l_gain, l_kw, l_vw, l_x, l_kc, l_vc, l_step, l_plan):
        cp.start()

    outs = []

    def out(src, dst):
        cp = pltpu.make_async_copy(src, dst, osem.at[len(outs)])
        cp.start()
        outs.append(cp)

    bar = pltpu.get_barrier_semaphore()
    peers = [sibling, right, left, dev(1, 0, c), dev(2, 0, c), dev(3, 0, c)] + partners
    for to in peers:
        pl.semaphore_signal(bar, inc=1, device_id=to, device_id_type=MESH)
    l_own = []
    for s in (2, 1, 3, 0):
        tx = lax.rem(xx + s, NX)
        for z in range(NZ):
            col = pl.multiple_of(((z * NX + tx) * 2 + c) * 128, 128)
            cp = local(
                act.at[:, pl.ds(col, 128)],
                x2h.at[s, pl.ds(pl.multiple_of(c * 512, 512), 512), pl.ds(z * 128, 128)],
                5 + s * 4 + z,
            )
            cp.start()
            l_own.append(cp)
    pl.semaphore_wait(bar, len(peers))

    l_gain.wait()
    l_kw.wait()
    l_vw.wait()
    gain_row = gain_ref[...]
    gain_col = jnp.transpose(jnp.broadcast_to(gain_row, (128, 128)))[:, 0:1]
    mine = gw.at[at(0, 0), pl.ds(pl.multiple_of(c * 128, 128), 128), :]
    mine[...] = (wv[...] * gain_col).astype(BF16)

    def piece(dz, dx):
        return gw.at[at(dz, dx), pl.ds(pl.multiple_of(c * 128, 128), 128), :]

    def sib_piece(dz, dx):
        return gw.at[at(dz, dx), pl.ds(pl.multiple_of(sib * 128, 128), 128), :]

    send(piece(0, 0), piece(0, 0), agsem.at[3], right)
    send(piece(0, 0), piece(0, 0), agsem.at[1], left)
    for dz in (1, 3, 2):
        send(piece(0, 0), piece(0, 0), agsem.at[(4 - dz) * 4], dev(dz, 0, c))

    for s in (2, 1, 3, 0):
        tx = lax.rem(xx + s, NX)
        for z in range(NZ):
            col = pl.multiple_of(((z * NX + tx) * 2 + sib) * 128, 128)
            send(
                act.at[:, pl.ds(col, 128)],
                x2h.at[s, pl.ds(pl.multiple_of(c * 512, 512), 512), pl.ds(z * 128, 128)],
                xsem.at[s],
                sibling,
            )
    send(piece(0, 0), piece(0, 0), sibsem.at[0], sibling)

    l_x.wait()
    l_kc.wait()
    l_vc.wait()

    @pl.loop(0, 4)
    def _(b):
        rows = pl.ds(pl.multiple_of(b * 128, 128), 128)
        xb = xv[rows, :].astype(F32)
        ms = jnp.sum(xb * xb, axis=-1, keepdims=True) * (1.0 / 4096.0)
        inv = lax.rsqrt(ms + 1e-05)
        inv_ref[rows, :] = jnp.broadcast_to(inv, (128, 128))
        lanes = pl.ds(pl.multiple_of(c * 512 + b * 128, 128), 128)
        for r in range(ROUNDS):
            ct = ctv[rows, r * KR : (r + 1) * KR].astype(F32) * inv
            ctT[r, :, lanes] = jnp.transpose(ct).astype(BF16)

    own_lanes = pl.ds(pl.multiple_of(c * 512, 512), 512)
    sib_lanes = pl.ds(pl.multiple_of(sib * 512, 512), 512)
    for r in range(ROUNDS):
        send(ctT.at[r, :, own_lanes], ctT.at[r, :, own_lanes], ctsem.at[r], sibling)
    for cp in l_own:
        cp.wait()

    def grad_block(r, s):
        res = jnp.dot(ctT[r], x2h[s], preferred_element_type=F32)
        for z in range(NZ):
            gs[r, s, z] = res[:, z * 128 : (z + 1) * 128].astype(BF16)

    HA = pl.ds(0, 2)
    HB = pl.ds(2, 2)

    def send_opp(r):
        grad_block(r, 2)
        send(gs.at[r, 2, HA], ropp.at[r, 0], oppsem.at[r * 2], right)
        send(gs.at[r, 2, HB], ropp.at[r, 1], oppsem.at[r * 2 + 1], left)

    def send_plain(r):
        send(gs.at[r, 1, HB], rpl.at[r, 0], plsem.at[r * 2], right)
        send(gs.at[r, 3, HA], rpl.at[r, 1], plsem.at[r * 2 + 1], left)

    def send_summed(r):
        arrived(ropp.at[r, 0], oppsem.at[r * 2])
        for h in range(2):
            gs[r, 1, h] = (gs[r, 1, h].astype(F32) + ropp[r, 0, h].astype(F32)).astype(BF16)
        send(gs.at[r, 1, HA], rsm.at[r, 0], smsem.at[r * 2], right)
        arrived(ropp.at[r, 1], oppsem.at[r * 2 + 1])
        for h in range(2):
            gs[r, 3, 2 + h] = (gs[r, 3, 2 + h].astype(F32) + ropp[r, 1, h].astype(F32)).astype(BF16)
        send(gs.at[r, 3, HB], rsm.at[r, 1], smsem.at[r * 2 + 1], left)

    def step(r):
        send_summed(r)
        if r + 1 < ROUNDS:
            send_plain(r + 1)
        if r + 2 < ROUNDS:
            send_opp(r + 2)
            grad_block(r + 2, 1)
            grad_block(r + 2, 3)
            grad_block(r + 2, 0)

    def x_total(r):
        arrived(rpl.at[r, 0], plsem.at[r * 2])
        arrived(rpl.at[r, 1], plsem.at[r * 2 + 1])
        arrived(rsm.at[r, 0], smsem.at[r * 2])
        arrived(rsm.at[r, 1], smsem.at[r * 2 + 1])
        for h in range(2):
            zs[r, h] = (
                gs[r, 0, h].astype(F32) + rsm[r, 0, h].astype(F32) + rpl[r, 1, h].astype(F32)
            ).astype(BF16)
            zs[r, 2 + h] = (
                gs[r, 0, 2 + h].astype(F32) + rpl[r, 0, h].astype(F32) + rsm[r, 1, h].astype(F32)
            ).astype(BF16)
        for dz in (1, 3, 2):
            send(
                zs.at[r, lax.rem(zh + dz, NZ)],
                rz.at[r, 3 - dz],
                zsem.at[r * 3 + 3 - dz],
                dev(dz, 0, c),
            )

    l_step.wait()
    l_plan.wait()
    hop = plan_ref[lax.rem(step_ref[0], 8)]
    gain_part = []

    def update(r):
        total = zs[r, zh].astype(F32)
        for i in range(3):
            arrived(rz.at[r, i], zsem.at[r * 3 + i])
            total = total + rz[r, i].astype(F32)
        grad = jnp.transpose(total) * (1.0 / 64.0)
        w = wv[:, r * KR : (r + 1) * KR]
        own[r, 0:128, :] = w - lr_weight * gain_col * grad
        gain_part.append(jnp.sum(w.astype(BF16).astype(F32) * grad, axis=-1, keepdims=True))
        if r < ROUNDS - 1:
            own[r, 128:144, :] = jnp.zeros((16, KR), F32)
        else:
            gain_sum = jnp.transpose(jnp.broadcast_to(sum(gain_part), (128, 128)))[0:1, :]
            new_gain = gain_row - lr_gain * gain_sum
            own[r, 128:144, :] = jnp.broadcast_to(
                jnp.concatenate([new_gain] * (KR // 128), axis=1), (16, KR)
            )
        psend[r, 0] = own[r].astype(BF16)
        for i in range(3):
            send(psend.at[r, 0], precv.at[r, i], psem.at[r * 4 + i], partners[i])

    def swap_y(r):
        v = psend[r, 0].astype(F32)
        low = hop % 4
        for i in range(3):
            arrived(precv.at[r, i], psem.at[r * 4 + i])
            v = jnp.where(low == i + 1, precv[r, i].astype(F32), v)
        psend[r, 1] = v.astype(BF16)
        send(psend.at[r, 1], precv.at[r, 3], psem.at[r * 4 + 3], partners[3])

    def swap_z(r):
        arrived(precv.at[r, 3], psem.at[r * 4 + 3])
        v = jnp.where(hop >= 4, precv[r, 3].astype(F32), psend[r, 1].astype(F32))
        o = own[r]
        avg = 0.5 * (o + jnp.where(hop == 0, o, v))
        nw_ref[:, r * KR : (r + 1) * KR] = avg[0:128]
        half = ROUNDS // 2
        if r == half - 1:
            out(nw_ref.at[:, pl.ds(0, 512)], nk_out.at[0])
        if r == ROUNDS - 1:
            out(nw_ref.at[:, pl.ds(512, 512)], nv_out.at[0])
            ng_ref[...] = avg[128:129, 0:128]
            out(ng_ref, ng_out)

    def rows_of(dz, dx, lo, n):
        return gw.at[at(dz, dx), pl.ds(pl.multiple_of(c * 128 + lo, 16), n), :]

    def forward_right(dz, lo, n):
        send(rows_of(dz, 3, lo, n), rows_of(dz, 3, lo, n), agsem.at[dz * 4 + 2], right)

    def forward_left(dz, lo, n):
        sem = agsem if n == 128 else agh
        k = dz * 4 + 2 if n == 128 else dz
        send(rows_of(dz, 1, lo, n), rows_of(dz, 1, lo, n), sem.at[k], left)

    def gathered(dz, dx):
        if dx == 2 and dz % 2 == 0:
            arrived(rows_of(dz, dx, 0, 64), agsem.at[dz * 4 + dx])
            arrived(rows_of(dz, dx, 64, 64), agh.at[dz])
        else:
            arrived(piece(dz, dx), agsem.at[dz * 4 + dx])
        send(piece(dz, dx), piece(dz, dx), sibsem.at[dz * 4 + dx], sibling)

    def pairs(first, items):
        for n, (dz, dx) in enumerate(items):
            arrived(sib_piece(dz, dx), sibsem.at[dz * 4 + dx])
        for n, (dz, dx) in enumerate(items):
            j = at(dz, dx)
            cols = pl.ds(pl.multiple_of(j * 256, 256), 256)

            @pl.loop(0, 2)
            def _(b):
                rows = pl.ds(pl.multiple_of(b * 256, 256), 256)
                part = jnp.dot(xv[rows, cols], gw[j], preferred_element_type=F32)
                if first and n == 0:
                    acc[rows, :] = part
                else:
                    acc[rows, :] += part
                d = lax.dot_general(
                    ctv[rows, :], gw[j], (((1,), (1,)), ((), ())), preferred_element_type=F32
                )
                dn_ref[rows, cols] = (d * (inv_ref[rows, 0:1] * (1.0 / 64.0))).astype(BF16)

            pltpu.make_async_copy(dn_ref.at[:, cols], dn_out.at[:, cols], dsem).start()

    for r in range(ROUNDS):
        arrived(ctT.at[r, :, sib_lanes], ctsem.at[r])
    for s in (2, 1, 3, 0):
        arrived(x2h.at[s, sib_lanes, :], xsem.at[s])
    send_opp(0)
    grad_block(0, 1)
    grad_block(0, 3)
    send_plain(0)
    send_opp(1)
    grad_block(1, 1)
    grad_block(1, 3)
    step(0)
    grad_block(0, 0)
    grad_block(1, 0)
    gathered(0, 1)
    gathered(0, 3)
    pairs(True, [(0, 0)])
    step(1)
    x_total(0)
    pairs(False, [(0, 1), (0, 3)])
    gathered(1, 0)
    gathered(3, 0)
    pairs(False, [(1, 0), (3, 0)])
    step(2)
    gathered(2, 0)
    update(0)
    x_total(1)
    pairs(False, [(2, 0)])
    swap_y(0)
    step(3)
    forward_left(0, 64, 64)
    forward_right(0, 0, 64)
    for dr, dl in ((1, 3), (2, 2), (3, 1)):
        send(piece(dr, 0), piece(dr, 0), agsem.at[dr * 4 + 3], right)
        send(piece(dl, 0), piece(dl, 0), agsem.at[dl * 4 + 1], left)
    swap_z(0)
    update(1)
    x_total(2)
    swap_y(1)
    x_total(3)
    swap_z(1)
    update(2)
    gathered(0, 2)
    pairs(False, [(0, 2)])
    swap_y(2)
    update(3)
    gathered(1, 3)
    forward_right(1, 0, 128)
    gathered(3, 1)
    forward_left(3, 0, 128)
    swap_z(2)
    pairs(False, [(1, 3), (3, 1)])
    swap_y(3)
    gathered(2, 3)
    forward_right(2, 0, 64)
    gathered(2, 1)
    forward_left(2, 64, 64)
    swap_z(3)
    pairs(False, [(2, 3), (2, 1)])
    gathered(3, 3)
    gathered(1, 1)
    pairs(False, [(3, 3), (1, 1)])
    gathered(1, 2)
    gathered(3, 2)
    pairs(False, [(1, 2), (3, 2)])
    gathered(2, 2)
    pairs(False, [(2, 2)])

    for b in range(4):
        rows = pl.ds(b * 128, 128)
        inv = inv_ref[rows, 0:1]
        kv = acc[rows, :] * (inv * (1.0 / 64.0))
        inner = jnp.sum(kv * ctv[rows, :].astype(F32), axis=-1, keepdims=True) * (1.0 / 4096.0)
        keys_ref[rows, :] = kv[:, 0:512].astype(BF16)
        values_ref[rows, :] = kv[:, 512:1024].astype(BF16)
        coef_ref[rows, :] = jnp.broadcast_to(inv * inv * inner, (128, 128))
        out(keys_ref.at[rows, :], keys_out.at[rows, :])
        out(values_ref.at[rows, :], values_out.at[rows, :])
        out(coef_ref.at[rows, :], coef_out.at[rows, :])

    for cp in sends:
        cp.wait_send()
    for cp in outs:
        cp.wait()
    pltpu.make_async_copy(dn_ref, dn_out, dsem).wait()


def body(
    activations,
    norm_gain,
    key_weight,
    value_weight,
    key_cotangent,
    value_cotangent,
    step_index,
    plan,
):
    hbm = pl.BlockSpec(memory_space=pltpu.HBM)
    shape = jax.ShapeDtypeStruct
    V = pltpu.VMEM
    DMA = pltpu.SemaphoreType.DMA
    keys, values, dn, coef, nk, nv, ng = pl.pallas_call(
        kernel,
        name="group_step",
        out_shape=(
            shape((512, 512), BF16),
            shape((512, 512), BF16),
            shape((512, 4096), BF16),
            shape((512, 128), F32),
            shape((1, 128, 512), F32),
            shape((1, 128, 512), F32),
            shape((1, 128), F32),
        ),
        in_specs=[hbm] * 8,
        out_specs=(hbm,) * 7,
        scratch_shapes=[
            V((512, 512), BF16),
            V((512, 512), BF16),
            V((512, 4096), BF16),
            V((512, 128), F32),
            V((128, 1024), F32),
            V((1, 128), F32),
            V((512, 4096), BF16),
            V((4, 1024, 512), BF16),
            V((512, 1024), BF16),
            V((ROUNDS, KR, 1024), BF16),
            V((128, 1024), F32),
            V((16, 256, 1024), BF16),
            V((ROUNDS, 4, 4, KR, 128), BF16),
            V((ROUNDS, 2, 2, KR, 128), BF16),
            V((ROUNDS, 2, 2, KR, 128), BF16),
            V((ROUNDS, 2, 2, KR, 128), BF16),
            V((ROUNDS, 4, KR, 128), BF16),
            V((ROUNDS, 3, KR, 128), BF16),
            V((512, 1024), F32),
            V((1, 128), F32),
            pltpu.SMEM((1,), jnp.int32),
            pltpu.SMEM((8,), jnp.int32),
            V((512, 128), F32),
            V((ROUNDS, 144, KR), F32),
            V((ROUNDS, 2, 144, KR), BF16),
            V((ROUNDS, 4, 144, KR), BF16),
            DMA((N_SEND,)),
            DMA((24,)),
            DMA((4,)),
            DMA((ROUNDS,)),
            DMA((16,)),
            DMA((4,)),
            DMA((16,)),
            DMA((2 * ROUNDS,)),
            DMA((2 * ROUNDS,)),
            DMA((2 * ROUNDS,)),
            DMA((3 * ROUNDS,)),
            DMA((4 * ROUNDS,)),
            DMA,
            DMA((20,)),
        ],
        compiler_params=pltpu.CompilerParams(
            collective_id=0, has_side_effects=True, vmem_limit_bytes=58 << 20
        ),
        cost_estimate=pl.CostEstimate(
            flops=13_000_000_000, bytes_accessed=24 << 20, transcendentals=512
        ),
    )(
        activations,
        norm_gain,
        key_weight,
        value_weight,
        key_cotangent,
        value_cotangent,
        step_index,
        plan,
    )
    return finish(activations, dn, coef, keys, values, nk, nv, ng)


def finish_kernel(
    act, dn, coef, keys, values, nk, nv, ng, grad_o, k_o, v_o, nk_o, nv_o, ng_o,
    cv, dv, av, out, kb, vb, nkb, nvb, ngb, sem, rsem, wsem,
):
    def start(src, dst, s):
        cp = pltpu.make_async_copy(src, dst, s)
        cp.start()
        return cp

    l_coef = start(coef, cv, sem.at[5])
    reads = []
    for b in range(FINISH):
        rows = pl.ds(b * FROWS, FROWS)
        reads.append(
            (
                start(dn.at[rows, :], dv.at[rows, :], rsem.at[b]),
                start(act.at[rows, :], av.at[rows, :], rsem.at[FINISH + b]),
            )
        )
    through = [
        (start(src, mid, sem.at[i]), mid, dst)
        for i, (src, mid, dst) in enumerate(
            ((keys, kb, k_o), (values, vb, v_o), (nk, nkb, nk_o), (nv, nvb, nv_o), (ng, ngb, ng_o))
        )
    ]
    passed = []
    l_coef.wait()
    for b in range(FINISH):
        rows = pl.ds(b * FROWS, FROWS)
        for cp in reads[b]:
            cp.wait()
        x = av[rows, :].astype(F32)
        out[rows, :] = (dv[rows, :].astype(F32) - x * cv[rows, 0:1]).astype(BF16)
        passed.append(start(out.at[rows, :], grad_o.at[rows, :], wsem.at[b]))
        if b == FINISH // 2:
            for i, (cp, mid, dst) in enumerate(through):
                cp.wait()
                passed.append(start(mid, dst, wsem.at[FINISH + i]))
    for cp in passed:
        cp.wait()


def finish(act, dn, coef, keys, values, nk, nv, ng):
    hbm = pl.BlockSpec(memory_space=pltpu.HBM)
    shape = jax.ShapeDtypeStruct
    DMA = pltpu.SemaphoreType.DMA
    grad, k, v, nk, nv, ng = pl.pallas_call(
        finish_kernel,
        name="finish",
        in_specs=[hbm] * 8,
        out_specs=(hbm,) * 6,
        out_shape=(
            shape((512, 4096), BF16),
            shape((512, 512), BF16),
            shape((512, 512), BF16),
            shape((1, 128, 512), F32),
            shape((1, 128, 512), F32),
            shape((1, 128), F32),
        ),
        scratch_shapes=[
            pltpu.VMEM((512, 128), F32),
            pltpu.VMEM((512, 4096), BF16),
            pltpu.VMEM((512, 4096), BF16),
            pltpu.VMEM((512, 4096), BF16),
            pltpu.VMEM((512, 512), BF16),
            pltpu.VMEM((512, 512), BF16),
            pltpu.VMEM((1, 128, 512), F32),
            pltpu.VMEM((1, 128, 512), F32),
            pltpu.VMEM((1, 128), F32),
            DMA((6,)),
            DMA((2 * FINISH,)),
            DMA((FINISH + 5,)),
        ],
        compiler_params=pltpu.CompilerParams(vmem_limit_bytes=60 << 20),
        cost_estimate=pl.CostEstimate(
            flops=3 * 512 * 4096, bytes_accessed=16 << 20, transcendentals=0
        ),
    )(act, dn, coef, keys, values, nk, nv, ng)
    return k, v, grad, nk, nv, ng


def solution(mesh):
    in_specs = (
        P(("rep", "fsdp"), None),
        P("rep", "fsdp"),
        P("rep", "fsdp", None),
        P("rep", "fsdp", None),
        P(("rep", "fsdp"), None),
        P(("rep", "fsdp"), None),
        P(),
        P(),
    )
    out_specs = (
        P(("rep", "fsdp"), None),
        P(("rep", "fsdp"), None),
        P(("rep", "fsdp"), None),
        P("rep", "fsdp", None),
        P("rep", "fsdp", None),
        P("rep", "fsdp"),
    )
    return jax.shard_map(body, mesh=mesh, in_specs=in_specs, out_specs=out_specs, check_vma=False)
```

```python
import jax
import jax.numpy as jnp
from jax import lax
from jax.experimental import pallas as pl
from jax.experimental.pallas import tpu as pltpu
from jax.sharding import PartitionSpec as P

MESH = pl.DeviceIdType.MESH
F32 = jnp.float32
BF16 = jnp.bfloat16

lr_weight = 0.25
lr_gain = 0.005

FINISH = 8
FROWS = 512 // FINISH
NX = 4
NZ = 4
N_SEND = 128
ROUNDS = 4
KR = 1024 // ROUNDS


def kernel(
    act,
    gain_in,
    kw,
    vw,
    kc,
    vc,
    step_in,
    plan_in,
    keys_out,
    values_out,
    dn_out,
    coef_out,
    nk_out,
    nv_out,
    ng_out,
    keys_ref,
    values_ref,
    dn_ref,
    coef_ref,
    nw_ref,
    ng_ref,
    xv,
    x2h,
    ctv,
    ctT,
    wv,
    gw,
    gs,
    ropp,
    rpl,
    rsm,
    zs,
    rz,
    acc,
    gain_ref,
    step_ref,
    plan_ref,
    inv_ref,
    own,
    psend,
    precv,
    ssem,
    lsem,
    xsem,
    ctsem,
    agsem,
    agh,
    sibsem,
    oppsem,
    plsem,
    smsem,
    zsem,
    psem,
    dsem,
    osem,
):
    me = lax.axis_index("fsdp")
    rep = lax.axis_index("rep")
    zh = me // 8
    xx = (me // 2) % 4
    c = me % 2
    sib = 1 - c

    def at(dz, dx):
        return lax.rem(zh + dz, NZ) * NX + lax.rem(xx + dx, NX)

    def dev(dz, dx, core):
        return (rep, at(dz, dx) * 2 + core)

    sibling = dev(0, 0, sib)
    right = dev(0, 1, c)
    left = dev(0, 3, c)
    bit0, bit1, bit2 = rep % 2, (rep // 2) % 2, (rep // 4) % 2
    partners = [
        (rep + 1 - 2 * bit0, me),
        (rep + 2 - 4 * bit1, me),
        (rep + 3 - 2 * bit0 - 4 * bit1, me),
        (rep + 4 - 8 * bit2, me),
    ]
    sends = []

    def send(src, dst, sem, to):
        cp = pltpu.make_async_remote_copy(
            src_ref=src,
            dst_ref=dst,
            send_sem=ssem.at[len(sends)],
            recv_sem=sem,
            device_id=to,
            device_id_type=MESH,
        )
        cp.start()
        sends.append(cp)

    def arrived(dst, sem):
        pltpu.make_async_remote_copy(
            src_ref=dst,
            dst_ref=dst,
            send_sem=ssem.at[0],
            recv_sem=sem,
            device_id=sibling,
            device_id_type=MESH,
        ).wait_recv()

    def local(src, dst, i):
        return pltpu.make_async_copy(src, dst, lsem.at[i])

    l_kw = local(kw.at[0], wv.at[:, pl.ds(0, 512)], 0)
    l_vw = local(vw.at[0], wv.at[:, pl.ds(512, 512)], 1)
    l_x = local(act, xv, 2)
    l_kc = local(kc, ctv.at[:, pl.ds(0, 512)], 3)
    l_vc = local(vc, ctv.at[:, pl.ds(512, 512)], 4)
    l_gain = local(gain_in, gain_ref, 21)
    l_step = local(step_in, step_ref, 22)
    l_plan = local(plan_in, plan_ref, 23)
    for cp in (l_gain, l_kw, l_vw, l_x, l_kc, l_vc, l_step, l_plan):
        cp.start()

    outs = []

    def out(src, dst):
        cp = pltpu.make_async_copy(src, dst, osem.at[len(outs)])
        cp.start()
        outs.append(cp)

    bar = pltpu.get_barrier_semaphore()
    peers = [sibling, right, left, dev(1, 0, c), dev(2, 0, c), dev(3, 0, c)] + partners
    for to in peers:
        pl.semaphore_signal(bar, inc=1, device_id=to, device_id_type=MESH)
    l_own = []
    for s in (2, 1, 3, 0):
        tx = lax.rem(xx + s, NX)
        for z in range(NZ):
            col = pl.multiple_of(((z * NX + tx) * 2 + c) * 128, 128)
            cp = local(
                act.at[:, pl.ds(col, 128)],
                x2h.at[s, pl.ds(pl.multiple_of(c * 512, 512), 512), pl.ds(z * 128, 128)],
                5 + s * 4 + z,
            )
            cp.start()
            l_own.append(cp)
    pl.semaphore_wait(bar, len(peers))

    l_gain.wait()
    l_kw.wait()
    l_vw.wait()
    gain_row = gain_ref[...]
    gain_col = jnp.transpose(jnp.broadcast_to(gain_row, (128, 128)))[:, 0:1]
    mine = gw.at[at(0, 0), pl.ds(pl.multiple_of(c * 128, 128), 128), :]
    mine[...] = (wv[...] * gain_col).astype(BF16)

    def piece(dz, dx):
        return gw.at[at(dz, dx), pl.ds(pl.multiple_of(c * 128, 128), 128), :]

    def sib_piece(dz, dx):
        return gw.at[at(dz, dx), pl.ds(pl.multiple_of(sib * 128, 128), 128), :]

    send(piece(0, 0), piece(0, 0), agsem.at[3], right)
    send(piece(0, 0), piece(0, 0), agsem.at[1], left)
    for dz in (1, 3, 2):
        send(piece(0, 0), piece(0, 0), agsem.at[(4 - dz) * 4], dev(dz, 0, c))

    for s in (2, 1, 3, 0):
        tx = lax.rem(xx + s, NX)
        for z in range(NZ):
            col = pl.multiple_of(((z * NX + tx) * 2 + sib) * 128, 128)
            send(
                act.at[:, pl.ds(col, 128)],
                x2h.at[s, pl.ds(pl.multiple_of(c * 512, 512), 512), pl.ds(z * 128, 128)],
                xsem.at[s],
                sibling,
            )
    send(piece(0, 0), piece(0, 0), sibsem.at[0], sibling)

    l_x.wait()
    l_kc.wait()
    l_vc.wait()

    @pl.loop(0, 4)
    def _(b):
        rows = pl.ds(pl.multiple_of(b * 128, 128), 128)
        xb = xv[rows, :].astype(F32)
        ms = jnp.sum(xb * xb, axis=-1, keepdims=True) * (1.0 / 4096.0)
        inv = lax.rsqrt(ms + 1e-05)
        inv_ref[rows, :] = jnp.broadcast_to(inv, (128, 128))
        lanes = pl.ds(pl.multiple_of(c * 512 + b * 128, 128), 128)
        for r in range(ROUNDS):
            ct = ctv[rows, r * KR : (r + 1) * KR].astype(F32) * inv
            ctT[r, :, lanes] = jnp.transpose(ct).astype(BF16)

    own_lanes = pl.ds(pl.multiple_of(c * 512, 512), 512)
    sib_lanes = pl.ds(pl.multiple_of(sib * 512, 512), 512)
    for r in range(ROUNDS):
        send(ctT.at[r, :, own_lanes], ctT.at[r, :, own_lanes], ctsem.at[r], sibling)
    for cp in l_own:
        cp.wait()

    def grad_block(r, s):
        res = jnp.dot(ctT[r], x2h[s], preferred_element_type=F32)
        for z in range(NZ):
            gs[r, s, z] = res[:, z * 128 : (z + 1) * 128].astype(BF16)

    HA = pl.ds(0, 2)
    HB = pl.ds(2, 2)

    def send_opp(r):
        grad_block(r, 2)
        send(gs.at[r, 2, HA], ropp.at[r, 0], oppsem.at[r * 2], right)
        send(gs.at[r, 2, HB], ropp.at[r, 1], oppsem.at[r * 2 + 1], left)

    def send_plain(r):
        send(gs.at[r, 1, HB], rpl.at[r, 0], plsem.at[r * 2], right)
        send(gs.at[r, 3, HA], rpl.at[r, 1], plsem.at[r * 2 + 1], left)

    def send_summed(r):
        arrived(ropp.at[r, 0], oppsem.at[r * 2])
        for h in range(2):
            gs[r, 1, h] = (gs[r, 1, h].astype(F32) + ropp[r, 0, h].astype(F32)).astype(BF16)
        send(gs.at[r, 1, HA], rsm.at[r, 0], smsem.at[r * 2], right)
        arrived(ropp.at[r, 1], oppsem.at[r * 2 + 1])
        for h in range(2):
            gs[r, 3, 2 + h] = (gs[r, 3, 2 + h].astype(F32) + ropp[r, 1, h].astype(F32)).astype(BF16)
        send(gs.at[r, 3, HB], rsm.at[r, 1], smsem.at[r * 2 + 1], left)

    def step(r):
        send_summed(r)
        if r + 1 < ROUNDS:
            send_plain(r + 1)
        if r + 2 < ROUNDS:
            send_opp(r + 2)
            grad_block(r + 2, 1)
            grad_block(r + 2, 3)
            grad_block(r + 2, 0)

    def x_total(r):
        arrived(rpl.at[r, 0], plsem.at[r * 2])
        arrived(rpl.at[r, 1], plsem.at[r * 2 + 1])
        arrived(rsm.at[r, 0], smsem.at[r * 2])
        arrived(rsm.at[r, 1], smsem.at[r * 2 + 1])
        for h in range(2):
            zs[r, h] = (
                gs[r, 0, h].astype(F32) + rsm[r, 0, h].astype(F32) + rpl[r, 1, h].astype(F32)
            ).astype(BF16)
            zs[r, 2 + h] = (
                gs[r, 0, 2 + h].astype(F32) + rpl[r, 0, h].astype(F32) + rsm[r, 1, h].astype(F32)
            ).astype(BF16)
        for dz in (1, 3, 2):
            send(
                zs.at[r, lax.rem(zh + dz, NZ)],
                rz.at[r, 3 - dz],
                zsem.at[r * 3 + 3 - dz],
                dev(dz, 0, c),
            )

    l_step.wait()
    l_plan.wait()
    hop = plan_ref[lax.rem(step_ref[0], 8)]
    gain_part = []

    def update(r):
        total = zs[r, zh].astype(F32)
        for i in range(3):
            arrived(rz.at[r, i], zsem.at[r * 3 + i])
            total = total + rz[r, i].astype(F32)
        grad = jnp.transpose(total) * (1.0 / 64.0)
        w = wv[:, r * KR : (r + 1) * KR]
        own[r, 0:128, :] = w - lr_weight * gain_col * grad
        gain_part.append(jnp.sum(w.astype(BF16).astype(F32) * grad, axis=-1, keepdims=True))
        if r < ROUNDS - 1:
            own[r, 128:144, :] = jnp.zeros((16, KR), F32)
        else:
            gain_sum = jnp.transpose(jnp.broadcast_to(sum(gain_part), (128, 128)))[0:1, :]
            new_gain = gain_row - lr_gain * gain_sum
            own[r, 128:144, :] = jnp.broadcast_to(
                jnp.concatenate([new_gain] * (KR // 128), axis=1), (16, KR)
            )
        psend[r, 0] = own[r].astype(BF16)
        for i in range(3):
            send(psend.at[r, 0], precv.at[r, i], psem.at[r * 4 + i], partners[i])

    def swap_y(r):
        v = psend[r, 0].astype(F32)
        low = hop % 4
        for i in range(3):
            arrived(precv.at[r, i], psem.at[r * 4 + i])
            v = jnp.where(low == i + 1, precv[r, i].astype(F32), v)
        psend[r, 1] = v.astype(BF16)
        send(psend.at[r, 1], precv.at[r, 3], psem.at[r * 4 + 3], partners[3])

    def swap_z(r):
        arrived(precv.at[r, 3], psem.at[r * 4 + 3])
        v = jnp.where(hop >= 4, precv[r, 3].astype(F32), psend[r, 1].astype(F32))
        o = own[r]
        avg = 0.5 * (o + jnp.where(hop == 0, o, v))
        nw_ref[:, r * KR : (r + 1) * KR] = avg[0:128]
        half = ROUNDS // 2
        if r == half - 1:
            out(nw_ref.at[:, pl.ds(0, 512)], nk_out.at[0])
        if r == ROUNDS - 1:
            out(nw_ref.at[:, pl.ds(512, 512)], nv_out.at[0])
            ng_ref[...] = avg[128:129, 0:128]
            out(ng_ref, ng_out)

    def rows_of(dz, dx, lo, n):
        return gw.at[at(dz, dx), pl.ds(pl.multiple_of(c * 128 + lo, 16), n), :]

    def forward_right(dz, lo, n):
        send(rows_of(dz, 3, lo, n), rows_of(dz, 3, lo, n), agsem.at[dz * 4 + 2], right)

    def forward_left(dz, lo, n):
        sem = agsem if n == 128 else agh
        k = dz * 4 + 2 if n == 128 else dz
        send(rows_of(dz, 1, lo, n), rows_of(dz, 1, lo, n), sem.at[k], left)

    def gathered(dz, dx):
        if dx == 2 and dz % 2 == 0:
            arrived(rows_of(dz, dx, 0, 64), agsem.at[dz * 4 + dx])
            arrived(rows_of(dz, dx, 64, 64), agh.at[dz])
        else:
            arrived(piece(dz, dx), agsem.at[dz * 4 + dx])
        send(piece(dz, dx), piece(dz, dx), sibsem.at[dz * 4 + dx], sibling)

    def back(j, cols):
        d = lax.dot_general(
            ctv[...], gw[j], (((1,), (1,)), ((), ())), preferred_element_type=F32
        )
        dn_ref[:, cols] = (d * (inv_ref[:, 0:1] * (1.0 / 64.0))).astype(BF16)
        pltpu.make_async_copy(dn_ref.at[:, cols], dn_out.at[:, cols], dsem).start()

    def pairs(first, items):
        for n, (dz, dx) in enumerate(items):
            arrived(sib_piece(dz, dx), sibsem.at[dz * 4 + dx])
        for n, (dz, dx) in enumerate(items):
            j = at(dz, dx)
            cols = pl.ds(pl.multiple_of(j * 256, 256), 256)

            back(j, cols)
            part = jnp.dot(xv[:, cols], gw[j], preferred_element_type=F32)
            if first and n == 0:
                acc[...] = part
            else:
                acc[...] += part

    for r in range(ROUNDS):
        arrived(ctT.at[r, :, sib_lanes], ctsem.at[r])
    for s in (2, 1, 3, 0):
        arrived(x2h.at[s, sib_lanes, :], xsem.at[s])
    send_opp(0)
    grad_block(0, 1)
    grad_block(0, 3)
    send_plain(0)
    send_opp(1)
    grad_block(1, 1)
    grad_block(1, 3)
    step(0)
    grad_block(0, 0)
    grad_block(1, 0)
    gathered(0, 1)
    gathered(0, 3)
    pairs(True, [(0, 0)])
    step(1)
    x_total(0)
    pairs(False, [(0, 1), (0, 3)])
    gathered(1, 0)
    gathered(3, 0)
    pairs(False, [(1, 0), (3, 0)])
    step(2)
    gathered(2, 0)
    update(0)
    x_total(1)
    pairs(False, [(2, 0)])
    swap_y(0)
    step(3)
    forward_left(0, 64, 64)
    forward_right(0, 0, 64)
    for dr, dl in ((1, 3), (2, 2), (3, 1)):
        send(piece(dr, 0), piece(dr, 0), agsem.at[dr * 4 + 3], right)
        send(piece(dl, 0), piece(dl, 0), agsem.at[dl * 4 + 1], left)
    swap_z(0)
    update(1)
    x_total(2)
    swap_y(1)
    x_total(3)
    swap_z(1)
    update(2)
    gathered(0, 2)
    pairs(False, [(0, 2)])
    swap_y(2)
    update(3)
    gathered(1, 3)
    forward_right(1, 0, 128)
    gathered(3, 1)
    forward_left(3, 0, 128)
    swap_z(2)
    pairs(False, [(1, 3), (3, 1)])
    gathered(2, 3)
    forward_right(2, 0, 64)
    gathered(2, 1)
    forward_left(2, 64, 64)
    pairs(False, [(2, 3), (2, 1)])
    gathered(3, 3)
    gathered(1, 1)
    pairs(False, [(3, 3), (1, 1)])
    swap_y(3)
    gathered(1, 2)
    gathered(3, 2)
    pairs(False, [(1, 2), (3, 2)])
    gathered(2, 2)
    arrived(sib_piece(2, 2), sibsem.at[10])
    last = at(2, 2)
    last_cols = pl.ds(pl.multiple_of(last * 256, 256), 256)

    for b in range(4):
        rows = pl.ds(b * 128, 128)
        inv = inv_ref[rows, 0:1]
        part = jnp.dot(xv[rows, last_cols], gw[last], preferred_element_type=F32)
        kv = (acc[rows, :] + part) * (inv * (1.0 / 64.0))
        inner = jnp.sum(kv * ctv[rows, :].astype(F32), axis=-1, keepdims=True) * (1.0 / 4096.0)
        keys_ref[rows, :] = kv[:, 0:512].astype(BF16)
        values_ref[rows, :] = kv[:, 512:1024].astype(BF16)
        coef_ref[rows, :] = jnp.broadcast_to(inv * inv * inner, (128, 128))
        out(keys_ref.at[rows, :], keys_out.at[rows, :])
        out(values_ref.at[rows, :], values_out.at[rows, :])
        out(coef_ref.at[rows, :], coef_out.at[rows, :])
    back(last, last_cols)
    swap_z(3)

    for cp in sends:
        cp.wait_send()
    for cp in outs:
        cp.wait()
    pltpu.make_async_copy(dn_ref, dn_out, dsem).wait()


def body(
    activations,
    norm_gain,
    key_weight,
    value_weight,
    key_cotangent,
    value_cotangent,
    step_index,
    plan,
):
    hbm = pl.BlockSpec(memory_space=pltpu.HBM)
    shape = jax.ShapeDtypeStruct
    V = pltpu.VMEM
    DMA = pltpu.SemaphoreType.DMA
    keys, values, dn, coef, nk, nv, ng = pl.pallas_call(
        kernel,
        name="group_step",
        out_shape=(
            shape((512, 512), BF16),
            shape((512, 512), BF16),
            shape((512, 4096), BF16),
            shape((512, 128), F32),
            shape((1, 128, 512), F32),
            shape((1, 128, 512), F32),
            shape((1, 128), F32),
        ),
        in_specs=[hbm] * 8,
        out_specs=(hbm,) * 7,
        scratch_shapes=[
            V((512, 512), BF16),
            V((512, 512), BF16),
            V((512, 4096), BF16),
            V((512, 128), F32),
            V((128, 1024), F32),
            V((1, 128), F32),
            V((512, 4096), BF16),
            V((4, 1024, 512), BF16),
            V((512, 1024), BF16),
            V((ROUNDS, KR, 1024), BF16),
            V((128, 1024), F32),
            V((16, 256, 1024), BF16),
            V((ROUNDS, 4, 4, KR, 128), BF16),
            V((ROUNDS, 2, 2, KR, 128), BF16),
            V((ROUNDS, 2, 2, KR, 128), BF16),
            V((ROUNDS, 2, 2, KR, 128), BF16),
            V((ROUNDS, 4, KR, 128), BF16),
            V((ROUNDS, 3, KR, 128), BF16),
            V((512, 1024), F32),
            V((1, 128), F32),
            pltpu.SMEM((1,), jnp.int32),
            pltpu.SMEM((8,), jnp.int32),
            V((512, 128), F32),
            V((ROUNDS, 144, KR), F32),
            V((ROUNDS, 2, 144, KR), BF16),
            V((ROUNDS, 4, 144, KR), BF16),
            DMA((N_SEND,)),
            DMA((24,)),
            DMA((4,)),
            DMA((ROUNDS,)),
            DMA((16,)),
            DMA((4,)),
            DMA((16,)),
            DMA((2 * ROUNDS,)),
            DMA((2 * ROUNDS,)),
            DMA((2 * ROUNDS,)),
            DMA((3 * ROUNDS,)),
            DMA((4 * ROUNDS,)),
            DMA,
            DMA((20,)),
        ],
        compiler_params=pltpu.CompilerParams(
            collective_id=0, has_side_effects=True, vmem_limit_bytes=58 << 20
        ),
        cost_estimate=pl.CostEstimate(
            flops=13_000_000_000, bytes_accessed=24 << 20, transcendentals=512
        ),
    )(
        activations,
        norm_gain,
        key_weight,
        value_weight,
        key_cotangent,
        value_cotangent,
        step_index,
        plan,
    )
    return finish(activations, dn, coef, keys, values, nk, nv, ng)


def finish_kernel(
    act, dn, coef, keys, values, nk, nv, ng, grad_o, k_o, v_o, nk_o, nv_o, ng_o,
    cv, dv, av, out, kb, vb, nkb, nvb, ngb, sem, rsem, wsem,
):
    def start(src, dst, s):
        cp = pltpu.make_async_copy(src, dst, s)
        cp.start()
        return cp

    l_coef = start(coef, cv, sem.at[5])
    reads = []
    for b in range(FINISH):
        rows = pl.ds(b * FROWS, FROWS)
        reads.append(
            (
                start(dn.at[rows, :], dv.at[rows, :], rsem.at[b]),
                start(act.at[rows, :], av.at[rows, :], rsem.at[FINISH + b]),
            )
        )
    through = [
        (start(src, mid, sem.at[i]), mid, dst)
        for i, (src, mid, dst) in enumerate(
            ((keys, kb, k_o), (values, vb, v_o), (nk, nkb, nk_o), (nv, nvb, nv_o), (ng, ngb, ng_o))
        )
    ]
    passed = []
    l_coef.wait()
    for b in range(FINISH):
        rows = pl.ds(b * FROWS, FROWS)
        for cp in reads[b]:
            cp.wait()
        x = av[rows, :].astype(F32)
        out[rows, :] = (dv[rows, :].astype(F32) - x * cv[rows, 0:1]).astype(BF16)
        passed.append(start(out.at[rows, :], grad_o.at[rows, :], wsem.at[b]))
        if b == FINISH // 2:
            for i, (cp, mid, dst) in enumerate(through):
                cp.wait()
                passed.append(start(mid, dst, wsem.at[FINISH + i]))
    for cp in passed:
        cp.wait()


def finish(act, dn, coef, keys, values, nk, nv, ng):
    hbm = pl.BlockSpec(memory_space=pltpu.HBM)
    shape = jax.ShapeDtypeStruct
    DMA = pltpu.SemaphoreType.DMA
    grad, k, v, nk, nv, ng = pl.pallas_call(
        finish_kernel,
        name="finish",
        in_specs=[hbm] * 8,
        out_specs=(hbm,) * 6,
        out_shape=(
            shape((512, 4096), BF16),
            shape((512, 512), BF16),
            shape((512, 512), BF16),
            shape((1, 128, 512), F32),
            shape((1, 128, 512), F32),
            shape((1, 128), F32),
        ),
        scratch_shapes=[
            pltpu.VMEM((512, 128), F32),
            pltpu.VMEM((512, 4096), BF16),
            pltpu.VMEM((512, 4096), BF16),
            pltpu.VMEM((512, 4096), BF16),
            pltpu.VMEM((512, 512), BF16),
            pltpu.VMEM((512, 512), BF16),
            pltpu.VMEM((1, 128, 512), F32),
            pltpu.VMEM((1, 128, 512), F32),
            pltpu.VMEM((1, 128), F32),
            DMA((6,)),
            DMA((2 * FINISH,)),
            DMA((FINISH + 5,)),
        ],
        compiler_params=pltpu.CompilerParams(vmem_limit_bytes=60 << 20),
        cost_estimate=pl.CostEstimate(
            flops=3 * 512 * 4096, bytes_accessed=16 << 20, transcendentals=0
        ),
    )(act, dn, coef, keys, values, nk, nv, ng)
    return k, v, grad, nk, nv, ng


def solution(mesh):
    in_specs = (
        P(("rep", "fsdp"), None),
        P("rep", "fsdp"),
        P("rep", "fsdp", None),
        P("rep", "fsdp", None),
        P(("rep", "fsdp"), None),
        P(("rep", "fsdp"), None),
        P(),
        P(),
    )
    out_specs = (
        P(("rep", "fsdp"), None),
        P(("rep", "fsdp"), None),
        P(("rep", "fsdp"), None),
        P("rep", "fsdp", None),
        P("rep", "fsdp", None),
        P("rep", "fsdp"),
    )
    return jax.shard_map(body, mesh=mesh, in_specs=in_specs, out_specs=out_specs, check_vma=False)
```

```python
import jax
import jax.numpy as jnp
from jax import lax
from jax.experimental import pallas as pl
from jax.experimental.pallas import tpu as pltpu
from jax.sharding import PartitionSpec as P

MESH = pl.DeviceIdType.MESH
F32 = jnp.float32
BF16 = jnp.bfloat16

lr_weight = 0.25
lr_gain = 0.005

FINISH = 8
AHEAD = 8
FROWS = 512 // FINISH
NX = 4
NZ = 4
N_SEND = 128
ROUNDS = 4
KR = 1024 // ROUNDS


def kernel(
    act,
    gain_in,
    kw,
    vw,
    kc,
    vc,
    step_in,
    plan_in,
    keys_out,
    values_out,
    dn_out,
    coef_out,
    nk_out,
    nv_out,
    ng_out,
    keys_ref,
    values_ref,
    dn_ref,
    coef_ref,
    nw_ref,
    ng_ref,
    xv,
    x2h,
    ctv,
    ctT,
    wv,
    gw,
    gs,
    ropp,
    rpl,
    rsm,
    zs,
    rz,
    acc,
    gain_ref,
    step_ref,
    plan_ref,
    inv_ref,
    own,
    psend,
    precv,
    ssem,
    lsem,
    xsem,
    ctsem,
    agsem,
    agh,
    sibsem,
    oppsem,
    plsem,
    smsem,
    zsem,
    psem,
    dsem,
    osem,
):
    me = lax.axis_index("fsdp")
    rep = lax.axis_index("rep")
    zh = me // 8
    xx = (me // 2) % 4
    c = me % 2
    sib = 1 - c

    def at(dz, dx):
        return lax.rem(zh + dz, NZ) * NX + lax.rem(xx + dx, NX)

    def dev(dz, dx, core):
        return (rep, at(dz, dx) * 2 + core)

    sibling = dev(0, 0, sib)
    right = dev(0, 1, c)
    left = dev(0, 3, c)
    bit0, bit1, bit2 = rep % 2, (rep // 2) % 2, (rep // 4) % 2
    partners = [
        (rep + 1 - 2 * bit0, me),
        (rep + 2 - 4 * bit1, me),
        (rep + 3 - 2 * bit0 - 4 * bit1, me),
        (rep + 4 - 8 * bit2, me),
    ]
    sends = []

    def send(src, dst, sem, to):
        cp = pltpu.make_async_remote_copy(
            src_ref=src,
            dst_ref=dst,
            send_sem=ssem.at[len(sends)],
            recv_sem=sem,
            device_id=to,
            device_id_type=MESH,
        )
        cp.start()
        sends.append(cp)

    def arrived(dst, sem):
        pltpu.make_async_remote_copy(
            src_ref=dst,
            dst_ref=dst,
            send_sem=ssem.at[0],
            recv_sem=sem,
            device_id=sibling,
            device_id_type=MESH,
        ).wait_recv()

    def local(src, dst, i):
        return pltpu.make_async_copy(src, dst, lsem.at[i])

    l_kw = local(kw.at[0], wv.at[:, pl.ds(0, 512)], 0)
    l_vw = local(vw.at[0], wv.at[:, pl.ds(512, 512)], 1)
    l_x = local(act, xv, 2)
    l_kc = local(kc, ctv.at[:, pl.ds(0, 512)], 3)
    l_vc = local(vc, ctv.at[:, pl.ds(512, 512)], 4)
    l_gain = local(gain_in, gain_ref, 21)
    l_step = local(step_in, step_ref, 22)
    l_plan = local(plan_in, plan_ref, 23)
    for cp in (l_gain, l_kw, l_vw, l_x, l_kc, l_vc, l_step, l_plan):
        cp.start()

    outs = []

    def out(src, dst):
        cp = pltpu.make_async_copy(src, dst, osem.at[len(outs)])
        cp.start()
        outs.append(cp)

    bar = pltpu.get_barrier_semaphore()
    peers = [sibling, right, left, dev(1, 0, c), dev(2, 0, c), dev(3, 0, c)] + partners
    for to in peers:
        pl.semaphore_signal(bar, inc=1, device_id=to, device_id_type=MESH)
    l_own = []
    for s in (2, 1, 3, 0):
        tx = lax.rem(xx + s, NX)
        for z in range(NZ):
            col = pl.multiple_of(((z * NX + tx) * 2 + c) * 128, 128)
            cp = local(
                act.at[:, pl.ds(col, 128)],
                x2h.at[s, pl.ds(pl.multiple_of(c * 512, 512), 512), pl.ds(z * 128, 128)],
                5 + s * 4 + z,
            )
            cp.start()
            l_own.append(cp)
    pl.semaphore_wait(bar, len(peers))

    l_gain.wait()
    l_kw.wait()
    l_vw.wait()
    gain_row = gain_ref[...]
    gain_col = jnp.transpose(jnp.broadcast_to(gain_row, (128, 128)))[:, 0:1]
    mine = gw.at[at(0, 0), pl.ds(pl.multiple_of(c * 128, 128), 128), :]
    mine[...] = (wv[...] * gain_col).astype(BF16)

    def piece(dz, dx):
        return gw.at[at(dz, dx), pl.ds(pl.multiple_of(c * 128, 128), 128), :]

    def sib_piece(dz, dx):
        return gw.at[at(dz, dx), pl.ds(pl.multiple_of(sib * 128, 128), 128), :]

    send(piece(0, 0), piece(0, 0), agsem.at[3], right)
    send(piece(0, 0), piece(0, 0), agsem.at[1], left)
    for dz in (1, 3, 2):
        send(piece(0, 0), piece(0, 0), agsem.at[(4 - dz) * 4], dev(dz, 0, c))

    for s in (2, 1, 3, 0):
        tx = lax.rem(xx + s, NX)
        for z in range(NZ):
            col = pl.multiple_of(((z * NX + tx) * 2 + sib) * 128, 128)
            send(
                act.at[:, pl.ds(col, 128)],
                x2h.at[s, pl.ds(pl.multiple_of(c * 512, 512), 512), pl.ds(z * 128, 128)],
                xsem.at[s],
                sibling,
            )
    send(piece(0, 0), piece(0, 0), sibsem.at[0], sibling)

    l_x.wait()
    l_kc.wait()
    l_vc.wait()

    @pl.loop(0, 4)
    def _(b):
        rows = pl.ds(pl.multiple_of(b * 128, 128), 128)
        xb = xv[rows, :].astype(F32)
        ms = jnp.sum(xb * xb, axis=-1, keepdims=True) * (1.0 / 4096.0)
        inv = lax.rsqrt(ms + 1e-05)
        inv_ref[rows, :] = jnp.broadcast_to(inv, (128, 128))

    own_lanes = pl.ds(pl.multiple_of(c * 512, 512), 512)
    sib_lanes = pl.ds(pl.multiple_of(sib * 512, 512), 512)

    def turn(r):
        @pl.loop(0, 4)
        def _(b):
            rows = pl.ds(pl.multiple_of(b * 128, 128), 128)
            lanes = pl.ds(pl.multiple_of(c * 512 + b * 128, 128), 128)
            ct = ctv[rows, r * KR : (r + 1) * KR].astype(F32) * inv_ref[rows, 0:1]
            ctT[r, :, lanes] = jnp.transpose(ct).astype(BF16)

        send(ctT.at[r, :, own_lanes], ctT.at[r, :, own_lanes], ctsem.at[r], sibling)

    turn(0)
    turn(1)
    for cp in l_own:
        cp.wait()

    def grad_block(r, s):
        res = jnp.dot(ctT[r], x2h[s], preferred_element_type=F32)
        for z in range(NZ):
            gs[r, s, z] = res[:, z * 128 : (z + 1) * 128].astype(BF16)

    HA = pl.ds(0, 2)
    HB = pl.ds(2, 2)

    def send_opp(r):
        grad_block(r, 2)
        send(gs.at[r, 2, HA], ropp.at[r, 0], oppsem.at[r * 2], right)
        send(gs.at[r, 2, HB], ropp.at[r, 1], oppsem.at[r * 2 + 1], left)

    def send_plain(r):
        send(gs.at[r, 1, HB], rpl.at[r, 0], plsem.at[r * 2], right)
        send(gs.at[r, 3, HA], rpl.at[r, 1], plsem.at[r * 2 + 1], left)

    def send_summed(r):
        arrived(ropp.at[r, 0], oppsem.at[r * 2])
        for h in range(2):
            gs[r, 1, h] = (gs[r, 1, h].astype(F32) + ropp[r, 0, h].astype(F32)).astype(BF16)
        send(gs.at[r, 1, HA], rsm.at[r, 0], smsem.at[r * 2], right)
        arrived(ropp.at[r, 1], oppsem.at[r * 2 + 1])
        for h in range(2):
            gs[r, 3, 2 + h] = (gs[r, 3, 2 + h].astype(F32) + ropp[r, 1, h].astype(F32)).astype(BF16)
        send(gs.at[r, 3, HB], rsm.at[r, 1], smsem.at[r * 2 + 1], left)

    def step(r):
        send_summed(r)
        if r + 1 < ROUNDS:
            send_plain(r + 1)
        if r + 2 < ROUNDS:
            send_opp(r + 2)
            grad_block(r + 2, 1)
            grad_block(r + 2, 3)
            grad_block(r + 2, 0)

    def x_total(r):
        arrived(rpl.at[r, 0], plsem.at[r * 2])
        arrived(rpl.at[r, 1], plsem.at[r * 2 + 1])
        arrived(rsm.at[r, 0], smsem.at[r * 2])
        arrived(rsm.at[r, 1], smsem.at[r * 2 + 1])
        for h in range(2):
            zs[r, h] = (
                gs[r, 0, h].astype(F32) + rsm[r, 0, h].astype(F32) + rpl[r, 1, h].astype(F32)
            ).astype(BF16)
            zs[r, 2 + h] = (
                gs[r, 0, 2 + h].astype(F32) + rpl[r, 0, h].astype(F32) + rsm[r, 1, h].astype(F32)
            ).astype(BF16)
        for dz in (1, 3, 2):
            send(
                zs.at[r, lax.rem(zh + dz, NZ)],
                rz.at[r, 3 - dz],
                zsem.at[r * 3 + 3 - dz],
                dev(dz, 0, c),
            )

    l_step.wait()
    l_plan.wait()
    hop = plan_ref[lax.rem(step_ref[0], 8)]
    gain_part = []

    def update(r):
        total = zs[r, zh].astype(F32)
        for i in range(3):
            arrived(rz.at[r, i], zsem.at[r * 3 + i])
            total = total + rz[r, i].astype(F32)
        grad = jnp.transpose(total) * (1.0 / 64.0)
        w = wv[:, r * KR : (r + 1) * KR]
        own[r, 0:128, :] = w - lr_weight * gain_col * grad
        gain_part.append(jnp.sum(w.astype(BF16).astype(F32) * grad, axis=-1, keepdims=True))
        if r < ROUNDS - 1:
            own[r, 128:144, :] = jnp.zeros((16, KR), F32)
        else:
            gain_sum = jnp.transpose(jnp.broadcast_to(sum(gain_part), (128, 128)))[0:1, :]
            new_gain = gain_row - lr_gain * gain_sum
            own[r, 128:144, :] = jnp.broadcast_to(
                jnp.concatenate([new_gain] * (KR // 128), axis=1), (16, KR)
            )
        psend[r, 0] = own[r].astype(BF16)
        for i in range(3):
            send(psend.at[r, 0], precv.at[r, i], psem.at[r * 4 + i], partners[i])

    def swap_y(r):
        v = psend[r, 0].astype(F32)
        low = hop % 4
        for i in range(3):
            arrived(precv.at[r, i], psem.at[r * 4 + i])
            v = jnp.where(low == i + 1, precv[r, i].astype(F32), v)
        psend[r, 1] = v.astype(BF16)
        send(psend.at[r, 1], precv.at[r, 3], psem.at[r * 4 + 3], partners[3])

    def swap_z(r):
        arrived(precv.at[r, 3], psem.at[r * 4 + 3])
        v = jnp.where(hop >= 4, precv[r, 3].astype(F32), psend[r, 1].astype(F32))
        o = own[r]
        avg = 0.5 * (o + jnp.where(hop == 0, o, v))
        nw_ref[:, r * KR : (r + 1) * KR] = avg[0:128]
        half = ROUNDS // 2
        if r == half - 1:
            out(nw_ref.at[:, pl.ds(0, 512)], nk_out.at[0])
        if r == ROUNDS - 1:
            out(nw_ref.at[:, pl.ds(512, 512)], nv_out.at[0])
            ng_ref[...] = avg[128:129, 0:128]
            out(ng_ref, ng_out)

    def rows_of(dz, dx, lo, n):
        return gw.at[at(dz, dx), pl.ds(pl.multiple_of(c * 128 + lo, 16), n), :]

    def forward_right(dz, lo, n):
        send(rows_of(dz, 3, lo, n), rows_of(dz, 3, lo, n), agsem.at[dz * 4 + 2], right)

    def forward_left(dz, lo, n):
        sem = agsem if n == 128 else agh
        k = dz * 4 + 2 if n == 128 else dz
        send(rows_of(dz, 1, lo, n), rows_of(dz, 1, lo, n), sem.at[k], left)

    def gathered(dz, dx):
        if dx == 2 and dz % 2 == 0:
            arrived(rows_of(dz, dx, 0, 64), agsem.at[dz * 4 + dx])
            arrived(rows_of(dz, dx, 64, 64), agh.at[dz])
        else:
            arrived(piece(dz, dx), agsem.at[dz * 4 + dx])
        send(piece(dz, dx), piece(dz, dx), sibsem.at[dz * 4 + dx], sibling)

    def back(j, cols):
        d = lax.dot_general(
            ctv[...], gw[j], (((1,), (1,)), ((), ())), preferred_element_type=F32
        )
        dn_ref[:, cols] = (d * (inv_ref[:, 0:1] * (1.0 / 64.0))).astype(BF16)
        pltpu.make_async_copy(dn_ref.at[:, cols], dn_out.at[:, cols], dsem).start()

    def pairs(first, items):
        for n, (dz, dx) in enumerate(items):
            arrived(sib_piece(dz, dx), sibsem.at[dz * 4 + dx])
        for n, (dz, dx) in enumerate(items):
            j = at(dz, dx)
            cols = pl.ds(pl.multiple_of(j * 256, 256), 256)

            back(j, cols)
            part = jnp.dot(xv[:, cols], gw[j], preferred_element_type=F32)
            if first and n == 0:
                acc[...] = part
            else:
                acc[...] += part

    def turned(r):
        arrived(ctT.at[r, :, sib_lanes], ctsem.at[r])

    def columns(t):
        arrived(x2h.at[t, sib_lanes, :], xsem.at[t])

    columns(2)
    turned(0)
    send_opp(0)
    columns(1)
    columns(3)
    grad_block(0, 1)
    grad_block(0, 3)
    send_plain(0)
    turned(1)
    send_opp(1)
    turn(2)
    turn(3)
    grad_block(1, 1)
    grad_block(1, 3)
    columns(0)
    turned(2)
    turned(3)
    step(0)
    grad_block(0, 0)
    grad_block(1, 0)
    gathered(0, 1)
    gathered(0, 3)
    pairs(True, [(0, 0)])
    step(1)
    x_total(0)
    pairs(False, [(0, 1), (0, 3)])
    gathered(1, 0)
    gathered(3, 0)
    pairs(False, [(1, 0), (3, 0)])
    step(2)
    gathered(2, 0)
    update(0)
    x_total(1)
    pairs(False, [(2, 0)])
    swap_y(0)
    step(3)
    early = len(sends)
    forward_left(0, 64, 64)
    forward_right(0, 0, 64)
    for dr, dl in ((1, 3), (2, 2), (3, 1)):
        send(piece(dr, 0), piece(dr, 0), agsem.at[dr * 4 + 3], right)
        send(piece(dl, 0), piece(dl, 0), agsem.at[dl * 4 + 1], left)
    swap_z(0)
    update(1)
    x_total(2)
    swap_y(1)
    x_total(3)
    swap_z(1)
    update(2)
    gathered(0, 2)
    pairs(False, [(0, 2)])
    swap_y(2)
    update(3)
    gathered(1, 3)
    forward_right(1, 0, 128)
    gathered(3, 1)
    forward_left(3, 0, 128)
    swap_z(2)
    pairs(False, [(1, 3), (3, 1)])
    gathered(2, 3)
    forward_right(2, 0, 64)
    gathered(2, 1)
    forward_left(2, 64, 64)
    pairs(False, [(2, 3), (2, 1)])
    gathered(3, 3)
    gathered(1, 1)
    pairs(False, [(3, 3), (1, 1)])
    swap_y(3)
    for cp in sends[:early]:
        cp.wait_send()
    gathered(1, 2)
    gathered(3, 2)
    pairs(False, [(1, 2), (3, 2)])
    gathered(2, 2)
    arrived(sib_piece(2, 2), sibsem.at[10])
    last = at(2, 2)
    last_cols = pl.ds(pl.multiple_of(last * 256, 256), 256)

    for b in range(4):
        rows = pl.ds(b * 128, 128)
        inv = inv_ref[rows, 0:1]
        part = jnp.dot(xv[rows, last_cols], gw[last], preferred_element_type=F32)
        kv = (acc[rows, :] + part) * (inv * (1.0 / 64.0))
        inner = jnp.sum(kv * ctv[rows, :].astype(F32), axis=-1, keepdims=True) * (1.0 / 4096.0)
        keys_ref[rows, :] = kv[:, 0:512].astype(BF16)
        values_ref[rows, :] = kv[:, 512:1024].astype(BF16)
        coef_ref[rows, :] = jnp.broadcast_to(inv * inv * inner, (128, 128))
        out(keys_ref.at[rows, :], keys_out.at[rows, :])
        out(values_ref.at[rows, :], values_out.at[rows, :])
        out(coef_ref.at[rows, :], coef_out.at[rows, :])
    back(last, last_cols)
    swap_z(3)

    for cp in sends[early:]:
        cp.wait_send()
    for cp in outs:
        cp.wait()
    pltpu.make_async_copy(dn_ref, dn_out, dsem).wait()


def body(
    activations,
    norm_gain,
    key_weight,
    value_weight,
    key_cotangent,
    value_cotangent,
    step_index,
    plan,
):
    hbm = pl.BlockSpec(memory_space=pltpu.HBM)
    shape = jax.ShapeDtypeStruct
    V = pltpu.VMEM
    DMA = pltpu.SemaphoreType.DMA
    keys, values, dn, coef, nk, nv, ng = pl.pallas_call(
        kernel,
        name="group_step",
        out_shape=(
            shape((512, 512), BF16),
            shape((512, 512), BF16),
            shape((512, 4096), BF16),
            shape((512, 128), F32),
            shape((1, 128, 512), F32),
            shape((1, 128, 512), F32),
            shape((1, 128), F32),
        ),
        in_specs=[hbm] * 8,
        out_specs=(hbm,) * 7,
        scratch_shapes=[
            V((512, 512), BF16),
            V((512, 512), BF16),
            V((512, 4096), BF16),
            V((512, 128), F32),
            V((128, 1024), F32),
            V((1, 128), F32),
            V((512, 4096), BF16),
            V((4, 1024, 512), BF16),
            V((512, 1024), BF16),
            V((ROUNDS, KR, 1024), BF16),
            V((128, 1024), F32),
            V((16, 256, 1024), BF16),
            V((ROUNDS, 4, 4, KR, 128), BF16),
            V((ROUNDS, 2, 2, KR, 128), BF16),
            V((ROUNDS, 2, 2, KR, 128), BF16),
            V((ROUNDS, 2, 2, KR, 128), BF16),
            V((ROUNDS, 4, KR, 128), BF16),
            V((ROUNDS, 3, KR, 128), BF16),
            V((512, 1024), F32),
            V((1, 128), F32),
            pltpu.SMEM((1,), jnp.int32),
            pltpu.SMEM((8,), jnp.int32),
            V((512, 128), F32),
            V((ROUNDS, 144, KR), F32),
            V((ROUNDS, 2, 144, KR), BF16),
            V((ROUNDS, 4, 144, KR), BF16),
            DMA((N_SEND,)),
            DMA((24,)),
            DMA((4,)),
            DMA((ROUNDS,)),
            DMA((16,)),
            DMA((4,)),
            DMA((16,)),
            DMA((2 * ROUNDS,)),
            DMA((2 * ROUNDS,)),
            DMA((2 * ROUNDS,)),
            DMA((3 * ROUNDS,)),
            DMA((4 * ROUNDS,)),
            DMA,
            DMA((20,)),
        ],
        compiler_params=pltpu.CompilerParams(
            collective_id=0, has_side_effects=True, vmem_limit_bytes=58 << 20
        ),
        cost_estimate=pl.CostEstimate(
            flops=13_000_000_000, bytes_accessed=24 << 20, transcendentals=512
        ),
    )(
        activations,
        norm_gain,
        key_weight,
        value_weight,
        key_cotangent,
        value_cotangent,
        step_index,
        plan,
    )
    return finish(activations, dn, coef, keys, values, nk, nv, ng)


def finish_kernel(
    act, dn, coef, keys, values, nk, nv, ng, grad_o, k_o, v_o, nk_o, nv_o, ng_o,
    cv, dv, av, out, kb, vb, nkb, nvb, ngb, sem, rsem, wsem,
):
    def start(src, dst, s):
        cp = pltpu.make_async_copy(src, dst, s)
        cp.start()
        return cp

    l_coef = start(coef, cv, sem.at[5])
    reads = []

    def read(b):
        rows = pl.ds(b * FROWS, FROWS)
        reads.append(
            (
                start(dn.at[rows, :], dv.at[rows, :], rsem.at[b]),
                start(act.at[rows, :], av.at[rows, :], rsem.at[FINISH + b]),
            )
        )
    through = [
        (start(src, mid, sem.at[i]), mid, dst)
        for i, (src, mid, dst) in enumerate(
            ((keys, kb, k_o), (values, vb, v_o), (nk, nkb, nk_o), (nv, nvb, nv_o), (ng, ngb, ng_o))
        )
    ]
    passed = []
    for b in range(AHEAD):
        read(b)
    l_coef.wait()
    for b in range(FINISH):
        rows = pl.ds(b * FROWS, FROWS)
        if b + AHEAD < FINISH:
            read(b + AHEAD)
        for cp in reads[b]:
            cp.wait()
        x = av[rows, :].astype(F32)
        out[rows, :] = (dv[rows, :].astype(F32) - x * cv[rows, 0:1]).astype(BF16)
        passed.append(start(out.at[rows, :], grad_o.at[rows, :], wsem.at[b]))
        if b == FINISH // 2:
            for i, (cp, mid, dst) in enumerate(through):
                cp.wait()
                passed.append(start(mid, dst, wsem.at[FINISH + i]))
    for cp in passed:
        cp.wait()


def finish(act, dn, coef, keys, values, nk, nv, ng):
    hbm = pl.BlockSpec(memory_space=pltpu.HBM)
    shape = jax.ShapeDtypeStruct
    DMA = pltpu.SemaphoreType.DMA
    grad, k, v, nk, nv, ng = pl.pallas_call(
        finish_kernel,
        name="finish",
        in_specs=[hbm] * 8,
        out_specs=(hbm,) * 6,
        out_shape=(
            shape((512, 4096), BF16),
            shape((512, 512), BF16),
            shape((512, 512), BF16),
            shape((1, 128, 512), F32),
            shape((1, 128, 512), F32),
            shape((1, 128), F32),
        ),
        scratch_shapes=[
            pltpu.VMEM((512, 128), F32),
            pltpu.VMEM((512, 4096), BF16),
            pltpu.VMEM((512, 4096), BF16),
            pltpu.VMEM((512, 4096), BF16),
            pltpu.VMEM((512, 512), BF16),
            pltpu.VMEM((512, 512), BF16),
            pltpu.VMEM((1, 128, 512), F32),
            pltpu.VMEM((1, 128, 512), F32),
            pltpu.VMEM((1, 128), F32),
            DMA((6,)),
            DMA((2 * FINISH,)),
            DMA((FINISH + 5,)),
        ],
        compiler_params=pltpu.CompilerParams(vmem_limit_bytes=60 << 20),
        cost_estimate=pl.CostEstimate(
            flops=3 * 512 * 4096, bytes_accessed=16 << 20, transcendentals=0
        ),
    )(act, dn, coef, keys, values, nk, nv, ng)
    return k, v, grad, nk, nv, ng


def solution(mesh):
    in_specs = (
        P(("rep", "fsdp"), None),
        P("rep", "fsdp"),
        P("rep", "fsdp", None),
        P("rep", "fsdp", None),
        P(("rep", "fsdp"), None),
        P(("rep", "fsdp"), None),
        P(),
        P(),
    )
    out_specs = (
        P(("rep", "fsdp"), None),
        P(("rep", "fsdp"), None),
        P(("rep", "fsdp"), None),
        P("rep", "fsdp", None),
        P("rep", "fsdp", None),
        P("rep", "fsdp"),
    )
    return jax.shard_map(body, mesh=mesh, in_specs=in_specs, out_specs=out_specs, check_vma=False)
```
